32 devices in a mesh: groups: 2 (over y), dp: 4 (over z), feat: 2 (over core), ens: 2 (over x).
Axes of the slice: x: 2, y: 2, z: 4, core: 2. Of those that a mesh axis runs over, the one named last changes fastest.
Arguments:
- test_feat: bfloat16 [2, 64, 8192], P('ens', 'groups', 'dp'), parts along dimension 1, may hold values from -6 to 6
- kernel_inverse: bfloat16 [2, 8192, 8192], P('ens', 'dp', 'feat'), may hold values from -0.0625 to 0.0625
- train_feat: bfloat16 [2, 1024, 8192], P('ens', 'dp', 'feat'), may hold values from -0.0625 to 0.0625
- residual_weight: float32 [2, 1024], P('ens', 'dp'), may hold values from 0.05 to 1
Outputs:
- scores: float32 [64, 1024], P(('groups', 'feat', 'ens'), 'dp'), parts along dimension 0
The draws below stay inside these ranges and needn't reach their ends.
There are 2 independent parts, one for each index of `groups`. The reference program is written for one: setup_inputs(seed, part) draws one part's arguments, and reference() takes and returns one part's arrays. A program takes and returns all parts, laid end to end along the dimension named above; an argument that names none is the same for every part. Nothing has to cross between parts.
All inputs are finite; a program needn't handle non-finite values.
Results may differ from the reference program's by a relative error of at most 0.0029.
Values may be sent and summed in bfloat16 or wider, within the bound.
No kernel may reach another device: no remote copies, remote signals or barrier semaphores. Data moves between devices by JAX's collectives and lax.ppermute only.
A program may use at most 64 MiB of HBM per device.

```python
import math
import jax
import jax.numpy as jnp
from jax import lax

P_SIZE = 8192
MODELS = 2
TEST = 32
NTRAIN = 1024
N_DP = 4


def block_levels(rng, extent, shards, smallest, top_value):
    def one(axis_at, shards_of):
        heights = jax.random.uniform(jax.random.fold_in(jax.random.fold_in(rng, 6), axis_at), (shards_of,), jnp.float32, smallest / len(shards), top_value / len(shards))
        return jnp.repeat(jnp.exp(heights), extent[axis_at] // shards_of).reshape((-1,) + (1,) * (len(extent) - axis_at - 1))

    gain = one(*shards[0])
    for cut in shards[1:]:
        gain = gain * one(*cut)
    return gain


def gaussian(own_key, dims, scale, reach, shards=(), kind=jnp.bfloat16):
    level = block_levels(own_key, dims, shards, -0.22, 0.18) if shards else 1.0
    entries = jax.random.normal(own_key, dims, jnp.float32) * scale * level
    return jnp.minimum(jnp.maximum(entries, -reach), reach).astype(kind)


def setup_inputs(seed: int = 0, part: int = 0) -> dict:
    arg_keys = jax.random.split(jax.random.key(seed), 5)
    own_keys = jax.random.split(jax.random.fold_in(arg_keys[4], part), 5)
    return {
        "test_feat": gaussian(own_keys[0], (MODELS, TEST, P_SIZE), 1.0, 6.0, ((0, 2), (2, 4))),
        "kernel_inverse": gaussian(arg_keys[1], (MODELS, P_SIZE, P_SIZE), P_SIZE ** -0.5, 0.0625, ((0, 2), (1, 4), (2, 2))),
        "train_feat": gaussian(arg_keys[2], (MODELS, NTRAIN, P_SIZE), P_SIZE ** -0.5, 0.0625, ((0, 2), (1, 4), (2, 2))),
        "residual_weight": jnp.clip(jnp.exp(math.log(1.0) - 2.9957323 * jax.random.uniform(arg_keys[3], (MODELS, NTRAIN), jnp.float32) ** block_levels(arg_keys[3], (MODELS, NTRAIN), ((0, 2), (1, 4)), -0.2, 0.2)), 0.05, 1.0),
    }


def project(test_one, inverse_one):
    width = P_SIZE // N_DP

    def add_block(index, total):
        start = (index * width).astype(jnp.int32)
        left = lax.dynamic_slice_in_dim(test_one, start, width, 1)
        right = lax.dynamic_slice_in_dim(inverse_one, start, width, 0)
        term = jnp.dot(left, right, preferred_element_type=jnp.float32)
        return total + term

    total = lax.fori_loop(0, N_DP, add_block, jnp.zeros((TEST, P_SIZE), jnp.float32))
    return total.astype(jnp.bfloat16)


def reference(test_feat, kernel_inverse, train_feat, residual_weight):
    scores = jnp.zeros((TEST, NTRAIN), jnp.float32)
    for model in range(MODELS):
        projected = project(test_feat[model], kernel_inverse[model])
        raw = jnp.dot(projected, train_feat[model].T, preferred_element_type=jnp.float32)
        scores = scores + raw * residual_weight[model][None, :]
    return scores
```

```python
import functools

import jax
import jax.numpy as jnp
from jax import lax
from jax.experimental import pallas as pl
from jax.experimental.pallas import tpu as pltpu
from jax.sharding import PartitionSpec as P

VMEM = pl.BlockSpec(memory_space=pltpu.VMEM)
HBM = pl.BlockSpec(memory_space=pltpu.HBM)


def place(n):
    z = lax.axis_index("dp")
    near = (z >= n // 2).astype(jnp.int32)
    hub = (z == n // 2 - 1) | (z == n // 2)
    return hub, near


def half_kernel(n, who, chunks, test_ref, inverse_ref, out_ref, test_buf, buf, total, test_sem, sems):
    hub, near = place(n)
    if who == "ends":
        active, half = jnp.logical_not(hub), 1 - near
    elif who == "hubs":
        active, half = hub, near
    else:
        active, half = None, jnp.where(hub, 1 - near, near)
    rows, width = buf.shape[1:]

    def run():
        columns = pl.ds(pl.multiple_of(half * width, width), width)
        test_copy = pltpu.make_async_copy(test_ref.at[0], test_buf, test_sem)
        test_copy.start()
        copies = [
            pltpu.make_async_copy(inverse_ref.at[0, pl.ds(c * rows, rows), columns], buf.at[c], sems.at[c])
            for c in range(chunks)
        ]
        for copy in copies:
            copy.start()
        test_copy.wait()
        for c in range(chunks):
            copies[c].wait()
            term = jnp.dot(test_buf[:, c * rows : (c + 1) * rows], buf[c], preferred_element_type=jnp.float32)
            if c:
                term = total[...] + term
            if c < chunks - 1:
                total[...] = term
            else:
                out_ref[...] = term.astype(out_ref.dtype)

    if active is None:
        run()
    else:
        pl.when(active)(run)


def half_dot(n, who, out_dtype, test, inverse):
    tests, depth = test.shape[1:]
    width = inverse.shape[2] // 2
    rows = min(depth, 256)
    chunks = depth // rows
    return pl.pallas_call(
        functools.partial(half_kernel, n, who, chunks),
        in_specs=[HBM, HBM],
        out_specs=VMEM,
        out_shape=jax.ShapeDtypeStruct((tests, width), out_dtype),
        scratch_shapes=[
            pltpu.VMEM((tests, depth), test.dtype),
            pltpu.VMEM((chunks, rows, width), inverse.dtype),
            pltpu.VMEM((tests, width), jnp.float32),
            pltpu.SemaphoreType.DMA,
            pltpu.SemaphoreType.DMA((chunks,)),
        ],
        compiler_params=pltpu.CompilerParams(vmem_limit_bytes=52 * 2**20),
        cost_estimate=pl.CostEstimate(
            flops=2 * tests * depth * width, bytes_accessed=2 * depth * width, transcendentals=0
        ),
        name="half_" + who,
    )(test, inverse)


def score_kernel(n, parts, sum_ref, across_ref, back_ref, far_ref, train_ref, weight_ref, *rest):
    outs, raw, near_buf, far_buf = rest[:parts], rest[parts], rest[parts + 1], rest[parts + 2]
    hub, near = place(n)
    width = sum_ref.shape[1]

    def halves(near_half, far_half):
        def run():
            near_buf[...] = near_half[...]
            far_buf[...] = far_half[...]

        return run

    pl.when(hub)(halves(sum_ref, across_ref))
    pl.when(jnp.logical_not(hub))(halves(back_ref, far_ref))
    contract = (((1,), (1,)), ((), ()))

    def half_score(values, half):
        columns = pl.ds(pl.multiple_of(half * width, width), width)
        return lax.dot_general(values[...], train_ref[0, :, columns], contract, preferred_element_type=jnp.float32)

    raw[...] = (half_score(near_buf, near) + half_score(far_buf, 1 - near)) * weight_ref[...]
    me = lax.axis_index("feat")
    rows = outs[0].shape[0]
    for step, out in enumerate(outs):
        block = lax.rem(me + step, parts)
        out[...] = raw[pl.ds(pl.multiple_of(block * rows, rows), rows), :]


def score(n, parts, total, across, back, far, train, weight):
    tests, width = total.shape
    columns = train.shape[1]
    return pl.pallas_call(
        functools.partial(score_kernel, n, parts),
        in_specs=[VMEM] * 6,
        out_specs=[VMEM] * parts,
        out_shape=[jax.ShapeDtypeStruct((tests // parts, columns), jnp.float32)] * parts,
        scratch_shapes=[
            pltpu.VMEM((tests, columns), jnp.float32),
            pltpu.VMEM((tests, width), total.dtype),
            pltpu.VMEM((tests, width), total.dtype),
        ],
        compiler_params=pltpu.CompilerParams(vmem_limit_bytes=16 * 2**20),
        cost_estimate=pl.CostEstimate(
            flops=4 * tests * columns * width, bytes_accessed=4 * columns * width, transcendentals=0
        ),
        name="score",
    )(total, across, back, far, train, weight)


def split_kernel(axis, parts, *refs):
    terms, outs, total = refs[: -parts - 1], refs[-parts - 1 : -1], refs[-1]
    value = terms[0][...]
    for term in terms[1:]:
        value = value + term[...]
    total[...] = value
    me = lax.axis_index(axis)
    rows = outs[0].shape[0]
    for step, out in enumerate(outs):
        block = lax.rem(me + step, parts)
        out[...] = total[pl.ds(pl.multiple_of(block * rows, rows), rows), :]


def add_and_split(axis, parts, terms):
    rows, columns = terms[0].shape
    return pl.pallas_call(
        functools.partial(split_kernel, axis, parts),
        in_specs=[VMEM] * len(terms),
        out_specs=[VMEM] * parts,
        out_shape=[jax.ShapeDtypeStruct((rows // parts, columns), jnp.float32)] * parts,
        scratch_shapes=[pltpu.VMEM((rows, columns), jnp.float32)],
        compiler_params=pltpu.CompilerParams(vmem_limit_bytes=4 * 2**20),
        name="add_and_split",
    )(*terms)


def exchange(axis, parts, blocks):
    received = [
        lax.ppermute(block, axis, [(i, (i + step) % parts) for i in range(parts)])
        for step, block in list(enumerate(blocks))[1:]
    ]
    return [blocks[0], *received]


def line_shards(n, feats, models, test_feat, kernel_inverse, train_feat, residual_weight):
    left, right = n // 2 - 1, n // 2
    ends_far = half_dot(n, "ends", jnp.bfloat16, test_feat, kernel_inverse)
    far_in = [lax.ppermute(ends_far, "dp", [(left - m, right), (right + m, left)]) for m in range(1, left + 1)]
    second = half_dot(n, "both", jnp.bfloat16, test_feat, kernel_inverse)
    across_in = lax.ppermute(second, "dp", [(left, right), (right, left)])
    near_in = [lax.ppermute(second, "dp", [(left - m, left), (right + m, right)]) for m in range(1, left + 1)]
    own = half_dot(n, "hubs", jnp.float32, test_feat, kernel_inverse)
    total = own
    for term in [*far_in, across_in, *near_in]:
        total = total + term
    total = total.astype(jnp.bfloat16)
    far_out = [lax.ppermute(total, "dp", [(left, right + m), (right, left - m)]) for m in range(1, left + 1)]
    near_out = [lax.ppermute(total, "dp", [(left, left - m), (right, right + m)]) for m in range(1, left + 1)]
    across_out = lax.ppermute(total, "dp", [(left, right), (right, left)])
    blocks = score(n, feats, total, across_out, sum(near_out), sum(far_out), train_feat, residual_weight)
    terms = exchange("feat", feats, blocks)
    blocks = add_and_split("ens", models, terms)
    terms = exchange("ens", models, blocks)
    result = terms[0]
    for term in terms[1:]:
        result = result + term
    return result


def general_shards(test_feat, kernel_inverse, train_feat, residual_weight):
    partial_sum = jnp.dot(test_feat[0], kernel_inverse[0], preferred_element_type=jnp.float32)
    projected = lax.psum(partial_sum, "dp").astype(jnp.bfloat16)
    raw = jnp.einsum("tf,nf->tn", projected, train_feat[0], preferred_element_type=jnp.float32)
    totals = raw * residual_weight[0][None, :]
    return lax.psum_scatter(totals, ("feat", "ens"), scatter_dimension=0, tiled=True)


def solution(mesh):
    in_specs = (
        P("ens", "groups", "dp"),
        P("ens", "dp", "feat"),
        P("ens", "dp", "feat"),
        P("ens", "dp"),
    )
    out_specs = P(("groups", "feat", "ens"), "dp")
    line = mesh.shape["dp"]
    if line % 2 == 0 and line // 2 - 1 == 1:
        body = functools.partial(line_shards, line, mesh.shape["feat"], mesh.shape["ens"])
    else:
        body = general_shards
    return jax.shard_map(body, mesh=mesh, in_specs=in_specs, out_specs=out_specs, check_vma=False)
```

```python
import functools

import jax
import jax.numpy as jnp
from jax import lax
from jax.experimental import pallas as pl
from jax.experimental.pallas import tpu as pltpu
from jax.sharding import PartitionSpec as P

VMEM = pl.BlockSpec(memory_space=pltpu.VMEM)
ANY = pl.BlockSpec(memory_space=pl.ANY)
MIB = 2**20


def project_kernel(n, steps, chunks, test_ref, inverse_ref, *rest):
    outs, (test_buf, buf, total, test_sem, sems) = rest[: len(steps)], rest[len(steps) :]
    me = lax.axis_index("dp")
    rows = buf.shape[1]
    width = outs[0].shape[1]
    test_copy = pltpu.make_async_copy(test_ref.at[0], test_buf, test_sem)
    test_copy.start()
    starts = [pl.multiple_of(lax.bitwise_xor(me, step) * width, width) for step in steps]
    copies = [
        [
            pltpu.make_async_copy(
                inverse_ref.at[0, pl.ds(c * rows, rows), pl.ds(start, width)],
                buf.at[c, :, pl.ds(i * width, width)],
                sems.at[c, i],
            )
            for i, start in enumerate(starts)
        ]
        for c in range(chunks)
    ]
    for group in copies:
        for copy in group:
            copy.start()
    test_copy.wait()
    for c in range(chunks):
        for copy in copies[c]:
            copy.wait()
        term = jnp.dot(test_buf[:, c * rows : (c + 1) * rows], buf[c], preferred_element_type=jnp.float32)
        if c:
            term = total[...] + term
        if c < chunks - 1:
            total[...] = term
        else:
            for i, out in enumerate(outs):
                out[...] = term[:, i * width : (i + 1) * width].astype(out.dtype)


def project(n, steps, out_dtype, test, inverse):
    tests, depth = test.shape[1:]
    width = inverse.shape[2] // n
    rows = min(depth, 256)
    chunks = depth // rows
    wide = width * len(steps)
    return pl.pallas_call(
        functools.partial(project_kernel, n, steps, chunks),
        in_specs=[ANY, ANY],
        out_specs=[VMEM] * len(steps),
        out_shape=[jax.ShapeDtypeStruct((tests, width), out_dtype)] * len(steps),
        scratch_shapes=[
            pltpu.VMEM((tests, depth), test.dtype),
            pltpu.VMEM((chunks, rows, wide), inverse.dtype),
            pltpu.VMEM((tests, wide), jnp.float32),
            pltpu.SemaphoreType.DMA,
            pltpu.SemaphoreType.DMA((chunks, len(steps))),
        ],
        compiler_params=pltpu.CompilerParams(vmem_limit_bytes=52 * MIB),
        cost_estimate=pl.CostEstimate(
            flops=2 * tests * depth * wide, bytes_accessed=2 * depth * wide, transcendentals=0
        ),
        name="project",
    )(test, inverse)


def score_kernel(steps, parts, axes, *refs):
    count = len(steps)
    blocks, train_ref, weight_ref, outs, raw = refs[:count], refs[count], refs[count + 1], refs[count + 2 : -1], refs[-1]
    me = lax.axis_index("dp")
    width = blocks[0].shape[1]
    contract = (((1,), (1,)), ((), ()))
    value = None
    for step, block in zip(steps, blocks):
        columns = pl.ds(pl.multiple_of(lax.bitwise_xor(me, step) * width, width), width)
        term = lax.dot_general(block[...], train_ref[0, :, columns], contract, preferred_element_type=jnp.float32)
        value = term if value is None else value + term
    raw[...] = value * weight_ref[...]
    place = lax.axis_index(axes[0]) * (parts // lax.axis_size(axes[0])) + lax.axis_index(axes[1])
    rows = outs[0].shape[0]
    for step, out in enumerate(outs):
        out[...] = raw[pl.ds(pl.multiple_of(lax.bitwise_xor(place, step) * rows, rows), rows), :]


def score(n, parts, axes, blocks, train, weight):
    tests, width = blocks[0].shape
    columns = train.shape[1]
    return pl.pallas_call(
        functools.partial(score_kernel, range(n), parts, axes),
        in_specs=[VMEM] * (n + 2),
        out_specs=[VMEM] * parts,
        out_shape=[jax.ShapeDtypeStruct((tests // parts, columns), jnp.float32)] * parts,
        scratch_shapes=[pltpu.VMEM((tests, columns), jnp.float32)],
        compiler_params=pltpu.CompilerParams(vmem_limit_bytes=16 * MIB),
        cost_estimate=pl.CostEstimate(
            flops=2 * n * tests * columns * width, bytes_accessed=2 * n * columns * width, transcendentals=0
        ),
        name="score",
    )(*blocks, train, weight)


def swap(x, axes, n, step):
    return lax.ppermute(x, axes, [(i, i ^ step) for i in range(n)])


def line_shards(n, parts, axes, test_feat, kernel_inverse, train_feat, residual_weight):
    order = (3, 2, 1)
    away = project(n, order, jnp.bfloat16, test_feat, kernel_inverse)
    terms = [swap(block, "dp", n, step) for step, block in zip(order, away)]
    (own,) = project(n, (0,), jnp.float32, test_feat, kernel_inverse)
    total = own
    for term in terms:
        total = total + term
    total = total.astype(jnp.bfloat16)
    blocks = [total] + [swap(total, "dp", n, step) for step in range(1, n)]
    rows = score(n, parts, axes, blocks, train_feat, residual_weight)
    result = rows[0]
    for step in range(1, parts):
        result = result + swap(rows[step], axes, parts, step)
    return result


def general_shards(test_feat, kernel_inverse, train_feat, residual_weight):
    partial_sum = jnp.dot(test_feat[0], kernel_inverse[0], preferred_element_type=jnp.float32)
    projected = lax.psum(partial_sum, "dp").astype(jnp.bfloat16)
    raw = jnp.einsum("tf,nf->tn", projected, train_feat[0], preferred_element_type=jnp.float32)
    totals = raw * residual_weight[0][None, :]
    return lax.psum_scatter(totals, ("feat", "ens"), scatter_dimension=0, tiled=True)


def solution(mesh):
    in_specs = (
        P("ens", "groups", "dp"),
        P("ens", "dp", "feat"),
        P("ens", "dp", "feat"),
        P("ens", "dp"),
    )
    out_specs = P(("groups", "feat", "ens"), "dp")
    line, axes = mesh.shape["dp"], ("feat", "ens")
    parts = mesh.shape["feat"] * mesh.shape["ens"]
    if line == 4 and parts == 4:
        body = functools.partial(line_shards, line, parts, axes)
    else:
        body = general_shards
    return jax.shard_map(body, mesh=mesh, in_specs=in_specs, out_specs=out_specs, check_vma=False)
```

```python
import functools

import jax
import jax.numpy as jnp
from jax import lax
from jax.experimental import pallas as pl
from jax.experimental.pallas import tpu as pltpu
from jax.sharding import PartitionSpec as P

VMEM = pl.BlockSpec(memory_space=pltpu.VMEM)
ANY = pl.BlockSpec(memory_space=pl.ANY)
MIB = 2**20


def project_kernel(n, steps, chunks, test_ref, inverse_ref, *rest):
    outs, (test_buf, buf, total, test_sems, sems) = rest[: len(steps)], rest[len(steps) :]
    me = lax.axis_index("dp")
    rows = buf.shape[1]
    width = outs[0].shape[1]
    starts = [pl.multiple_of(lax.bitwise_xor(me, step) * width, width) for step in steps]
    copies = []
    for c in range(chunks):
        part = pl.ds(c * rows, rows)
        test_copy = pltpu.make_async_copy(test_ref.at[0, :, part], test_buf.at[:, part], test_sems.at[c])
        test_copy.start()
        copies.append([test_copy])
        for i, start in enumerate(starts):
            copy = pltpu.make_async_copy(
                inverse_ref.at[0, part, pl.ds(start, width)], buf.at[c, :, pl.ds(i * width, width)], sems.at[c, i]
            )
            copy.start(priority=1)
            copies[c].append(copy)
    for c in range(chunks):
        for copy in copies[c]:
            copy.wait()
        term = jnp.dot(test_buf[:, c * rows : (c + 1) * rows], buf[c], preferred_element_type=jnp.float32)
        if c:
            term = total[...] + term
        if c < chunks - 1:
            total[...] = term
        else:
            for i, out in enumerate(outs):
                out[...] = term[:, i * width : (i + 1) * width].astype(out.dtype)


def project(n, steps, out_dtype, test, inverse):
    tests, depth = test.shape[1:]
    width = inverse.shape[2] // n
    rows = min(depth, 256)
    chunks = depth // rows
    wide = width * len(steps)
    return pl.pallas_call(
        functools.partial(project_kernel, n, steps, chunks),
        in_specs=[ANY, ANY],
        out_specs=[VMEM] * len(steps),
        out_shape=[jax.ShapeDtypeStruct((tests, width), out_dtype)] * len(steps),
        scratch_shapes=[
            pltpu.VMEM((tests, depth), test.dtype),
            pltpu.VMEM((chunks, rows, wide), inverse.dtype),
            pltpu.VMEM((tests, wide), jnp.float32),
            pltpu.SemaphoreType.DMA((chunks,)),
            pltpu.SemaphoreType.DMA((chunks, len(steps))),
        ],
        compiler_params=pltpu.CompilerParams(vmem_limit_bytes=215 * MIB // 4),
        cost_estimate=pl.CostEstimate(
            flops=2 * tests * depth * wide, bytes_accessed=2 * depth * wide, transcendentals=0
        ),
        name="project",
    )(test, inverse)


def score_kernel(steps, parts, axes, *refs):
    count = len(steps)
    blocks, train_ref, refs = refs[:count], refs[count], refs[count + 1 :]
    me = lax.axis_index("dp")
    width = blocks[0].shape[1]
    contract = (((1,), (1,)), ((), ()))
    value = None
    for step, block in zip(steps, blocks):
        columns = pl.ds(pl.multiple_of(lax.bitwise_xor(me, step) * width, width), width)
        term = lax.dot_general(block[...], train_ref[0, :, columns], contract, preferred_element_type=jnp.float32)
        value = term if value is None else value + term
    if not parts:
        refs[0][...] = value
        return
    so_far, weight_ref, outs, raw = refs[0], refs[1], refs[2:-1], refs[-1]
    raw[...] = (so_far[...] + value) * weight_ref[...]
    place = lax.axis_index(axes[0]) * (parts // lax.axis_size(axes[0])) + lax.axis_index(axes[1])
    rows = outs[0].shape[0]
    for step, out in enumerate(outs):
        out[...] = raw[pl.ds(pl.multiple_of(lax.bitwise_xor(place, step) * rows, rows), rows), :]


def score(steps, parts, axes, blocks, train, *more):
    tests, width = blocks[0].shape
    columns = train.shape[1]
    count = len(blocks)
    out = [jax.ShapeDtypeStruct((tests // max(parts, 1), columns), jnp.float32)] * max(parts, 1)
    return pl.pallas_call(
        functools.partial(score_kernel, steps, parts, axes),
        in_specs=[VMEM] * (count + 1 + len(more)),
        out_specs=[VMEM] * len(out),
        out_shape=out,
        scratch_shapes=[pltpu.VMEM((tests, columns), jnp.float32)] * bool(parts),
        compiler_params=pltpu.CompilerParams(vmem_limit_bytes=16 * MIB),
        cost_estimate=pl.CostEstimate(
            flops=2 * count * tests * columns * width, bytes_accessed=2 * count * columns * width, transcendentals=0
        ),
        name="score",
    )(*blocks, train, *more)


def swap(x, axes, n, step):
    return lax.ppermute(x, axes, [(i, i ^ step) for i in range(n)])


def line_shards(n, parts, axes, test_feat, kernel_inverse, train_feat, residual_weight):
    order = (3, 2, 1)
    away = project(n, order, jnp.bfloat16, test_feat, kernel_inverse)
    sent = {step: swap(block, "dp", n, step) for step, block in zip(order, away)}
    (own,) = project(n, (0,), jnp.float32, test_feat, kernel_inverse)
    total = own
    for step in (3, 1, 2):
        total = total + sent[step]
    total = total.astype(jnp.bfloat16)
    back = (3, 2, 1)
    blocks = [total] + [swap(total, "dp", n, step) for step in back]
    first = 2
    (raw,) = score((0, *back)[:first], 0, axes, blocks[:first], train_feat)
    rows = score((0, *back)[first:], parts, axes, blocks[first:], train_feat, raw, residual_weight)
    result = rows[0]
    for step in (3, 1, 2):
        result = result + swap(rows[step], axes, parts, step)
    return result


def general_shards(test_feat, kernel_inverse, train_feat, residual_weight):
    partial_sum = jnp.dot(test_feat[0], kernel_inverse[0], preferred_element_type=jnp.float32)
    projected = lax.psum(partial_sum, "dp").astype(jnp.bfloat16)
    raw = jnp.einsum("tf,nf->tn", projected, train_feat[0], preferred_element_type=jnp.float32)
    totals = raw * residual_weight[0][None, :]
    return lax.psum_scatter(totals, ("feat", "ens"), scatter_dimension=0, tiled=True)


def solution(mesh):
    in_specs = (
        P("ens", "groups", "dp"),
        P("ens", "dp", "feat"),
        P("ens", "dp", "feat"),
        P("ens", "dp"),
    )
    out_specs = P(("groups", "feat", "ens"), "dp")
    line, axes = mesh.shape["dp"], ("feat", "ens")
    parts = mesh.shape["feat"] * mesh.shape["ens"]
    if line == 4 and parts == 4:
        body = functools.partial(line_shards, line, parts, axes)
    else:
        body = general_shards
    return jax.shard_map(body, mesh=mesh, in_specs=in_specs, out_specs=out_specs, check_vma=False)
```

```python
import functools

import jax
import jax.numpy as jnp
from jax import lax
from jax.experimental import pallas as pl
from jax.experimental.pallas import tpu as pltpu
from jax.sharding import PartitionSpec as P

VMEM = pl.BlockSpec(memory_space=pltpu.VMEM)
ANY = pl.BlockSpec(memory_space=pl.ANY)
MIB = 2**20
LANES = 128
SHORT_LINE = 4


def pick(table, z):
    value = table[0]
    for i, entry in enumerate(table[1:], 1):
        value = jnp.where(z == i, entry, value)
    return value


def sources(table):
    return tuple(table.index(i) for i in range(len(table)))


def plain_ring(n, step):
    return tuple((z + step) % n for z in range(n))


def folded_ring(n, step):
    ring = (0, *range(1, n, 2), *range(n - 2, 0, -2))
    return tuple(ring[(ring.index(z) + step) % n] for z in range(n))


def run_copies(copies, product, cuts, total):
    for c, (low, high) in enumerate(zip(cuts, cuts[1:])):
        for copy in copies[c]:
            copy.wait()
        term = product(low, high)
        total[...] = total[...] + term if c else term


def project_kernel(n, tables, cuts, test_ref, inverse_ref, *rest):
    outs, (test_buf, buf, total, test_sems, sems) = rest[:-5], rest[-5:]
    me = lax.axis_index("dp")
    width = outs[0].shape[1]
    half = n // 2
    near = me // half * half
    if tables:
        runs = [((half - near) * width, half * width)]
        runs += [((near + (me + j) % half) * width, width) for j in range(1, half)]
    else:
        runs = [(me * width, width)]
    copies = []
    for c, (low, high) in enumerate(zip(cuts, cuts[1:])):
        part = pl.ds(low, high - low)
        copies.append([pltpu.make_async_copy(test_ref.at[0, :, part], test_buf.at[:, part], test_sems.at[c])])
        copies[c][0].start()
        at = 0
        for i, (first, span) in enumerate(runs):
            source = inverse_ref.at[0, part, pl.ds(pl.multiple_of(first, span), span)]
            copies[c].append(pltpu.make_async_copy(source, buf.at[part, pl.ds(at, span)], sems.at[c, i]))
            copies[c][-1].start(priority=1)
            at += span

    def product(low, high):
        return jnp.dot(test_buf[:, low:high], buf[low:high, :], preferred_element_type=jnp.float32)

    run_copies(copies, product, cuts, total)
    if not tables:
        outs[0][...] = total[...]
        return
    for table, out in zip(tables, outs):
        block = pick(table, me)
        place = jnp.where(block // half == me // half, half + (block - me + half) % half - 1, block % half)
        out[...] = total[:, pl.ds(pl.multiple_of(place * width, width), width)].astype(out.dtype)


def project(n, tables, out_dtype, test, inverse):
    tests, depth = test.shape[1:]
    width = inverse.shape[2] // n
    count = max(len(tables), 1)
    runs = n // 2 if tables else 1
    rows = min(depth, 2 * LANES)
    cuts = list(range(0, depth, rows)) + [depth]
    if cuts[-1] - cuts[-2] == 2 * LANES:
        cuts.insert(-1, depth - LANES)
    return pl.pallas_call(
        functools.partial(project_kernel, n, tables, cuts),
        in_specs=[ANY, ANY],
        out_specs=[VMEM] * count,
        out_shape=[jax.ShapeDtypeStruct((tests, width), out_dtype)] * count,
        scratch_shapes=[
            pltpu.VMEM((tests, depth), test.dtype),
            pltpu.VMEM((depth, width * count), inverse.dtype),
            pltpu.VMEM((tests, width * count), jnp.float32),
            pltpu.SemaphoreType.DMA((len(cuts) - 1,)),
            pltpu.SemaphoreType.DMA((len(cuts) - 1, runs)),
        ],
        compiler_params=pltpu.CompilerParams(vmem_limit_bytes=215 * MIB // 4),
        cost_estimate=pl.CostEstimate(
            flops=2 * tests * depth * width * count, bytes_accessed=2 * depth * width * count, transcendentals=0
        ),
        name="project",
    )(test, inverse)


def score_kernel(tables, parts, axes, *refs):
    count = len(tables)
    blocks, train_ref, refs = refs[:count], refs[count], refs[count + 1 :]
    me = lax.axis_index("dp")
    width = blocks[0].shape[1]
    contract = (((1,), (1,)), ((), ()))
    value = None
    for table, block in zip(tables, blocks):
        columns = pl.ds(pl.multiple_of(pick(table, me) * width, width), width)
        term = lax.dot_general(block[...], train_ref[0, :, columns], contract, preferred_element_type=jnp.float32)
        value = term if value is None else value + term
    if not parts:
        refs[0][...] = value
        return
    so_far, weight_ref, outs, raw = refs[0], refs[1], refs[2:-1], refs[-1]
    raw[...] = (so_far[...] + value) * weight_ref[...]
    place = lax.axis_index(axes[0]) * lax.axis_size(axes[1]) + lax.axis_index(axes[1])
    rows = outs[0].shape[0]
    for step, out in enumerate(outs):
        out[...] = raw[pl.ds(pl.multiple_of(lax.bitwise_xor(place, step) * rows, rows), rows), :]


def score(tables, parts, axes, blocks, train, *more):
    tests, width = blocks[0].shape
    columns = train.shape[1]
    count = len(blocks)
    outs = max(parts, 1)
    return pl.pallas_call(
        functools.partial(score_kernel, tables, parts, axes),
        in_specs=[VMEM] * (count + 1 + len(more)),
        out_specs=[VMEM] * outs,
        out_shape=[jax.ShapeDtypeStruct((tests // outs, columns), jnp.float32)] * outs,
        scratch_shapes=[pltpu.VMEM((tests, columns), jnp.float32)] * bool(parts),
        compiler_params=pltpu.CompilerParams(vmem_limit_bytes=16 * MIB),
        cost_estimate=pl.CostEstimate(
            flops=2 * count * tests * columns * width, bytes_accessed=2 * count * columns * width, transcendentals=0
        ),
        name="score",
    )(*blocks, train, *more)


def send(x, axes, table):
    return lax.ppermute(x, axes, list(enumerate(table)))


def line_shards(n, parts, axes, test_feat, kernel_inverse, train_feat, residual_weight):
    out_tables = [folded_ring(n, step) for step in range(1, n)]
    away = project(n, out_tables, jnp.bfloat16, test_feat, kernel_inverse)
    terms = [send(block, "dp", table) for table, block in zip(out_tables, away)]
    (total,) = project(n, [], jnp.float32, test_feat, kernel_inverse)
    for term in terms:
        total = total + term
    total = total.astype(jnp.bfloat16)
    back_tables = [plain_ring(n, step) for step in range(1, n)]
    blocks = [total] + [send(total, "dp", table) for table in back_tables]
    owners = [plain_ring(n, 0)] + [sources(table) for table in back_tables]
    (raw,) = score(owners[:2], 0, axes, blocks[:2], train_feat)
    rows = score(owners[2:], parts, axes, blocks[2:], train_feat, raw, residual_weight)
    result = rows[0]
    for step in (parts - 1, *range(1, parts - 1)):
        result = result + send(rows[step], axes, [z ^ step for z in range(parts)])
    return result


def general_shards(test_feat, kernel_inverse, train_feat, residual_weight):
    partial_sum = jnp.dot(test_feat[0], kernel_inverse[0], preferred_element_type=jnp.float32)
    projected = lax.psum(partial_sum, "dp").astype(jnp.bfloat16)
    raw = jnp.einsum("tf,nf->tn", projected, train_feat[0], preferred_element_type=jnp.float32)
    totals = raw * residual_weight[0][None, :]
    return lax.psum_scatter(totals, ("feat", "ens"), scatter_dimension=0, tiled=True)


def solution(mesh):
    in_specs = (
        P("ens", "groups", "dp"),
        P("ens", "dp", "feat"),
        P("ens", "dp", "feat"),
        P("ens", "dp"),
    )
    out_specs = P(("groups", "feat", "ens"), "dp")
    line, axes = mesh.shape["dp"], ("feat", "ens")
    parts = mesh.shape["feat"] * mesh.shape["ens"]
    if 2 < line <= SHORT_LINE and line % 2 == 0 and parts > 2 and parts & (parts - 1) == 0:
        body = functools.partial(line_shards, line, parts, axes)
    else:
        body = general_shards
    return jax.shard_map(body, mesh=mesh, in_specs=in_specs, out_specs=out_specs, check_vma=False)
```

```python
import functools

import jax
import jax.numpy as jnp
from jax import lax
from jax.experimental import pallas as pl
from jax.experimental.pallas import tpu as pltpu
from jax.sharding import PartitionSpec as P

VMEM = pl.BlockSpec(memory_space=pltpu.VMEM)
ANY = pl.BlockSpec(memory_space=pl.ANY)
MIB = 2**20
LANES = 128
SHORT_LINE = 4


def pick(table, z):
    value = table[0]
    for i, entry in enumerate(table[1:], 1):
        value = jnp.where(z == i, entry, value)
    return value


def sources(table):
    return tuple(table.index(i) for i in range(len(table)))


def plain_ring(n, step):
    return tuple((z + step) % n for z in range(n))


def folded_ring(n, step):
    ring = (0, *range(1, n, 2), *range(n - 2, 0, -2))
    return tuple(ring[(ring.index(z) + step) % n] for z in range(n))


def run_copies(copies, product, cuts, total):
    for c, (low, high) in enumerate(zip(cuts, cuts[1:])):
        for copy in copies[c]:
            copy.wait()
        term = product(low, high)
        total[...] = total[...] + term if c else term


def project_kernel(n, tables, cuts, test_ref, inverse_ref, *rest):
    outs, (test_buf, buf, total, test_sems, sems) = rest[:-5], rest[-5:]
    me = lax.axis_index("dp")
    width = outs[0].shape[1]
    half = n // 2
    near = me // half * half
    if tables:
        runs = [((half - near) * width, half * width)]
        runs += [((near + (me + j) % half) * width, width) for j in range(1, half)]
    else:
        runs = [(me * width, width)]
    copies = []
    for c, (low, high) in enumerate(zip(cuts, cuts[1:])):
        part = pl.ds(low, high - low)
        copies.append([pltpu.make_async_copy(test_ref.at[0, :, part], test_buf.at[:, part], test_sems.at[c])])
        copies[c][0].start()
        at = 0
        for i, (first, span) in enumerate(runs):
            source = inverse_ref.at[0, part, pl.ds(pl.multiple_of(first, span), span)]
            copies[c].append(pltpu.make_async_copy(source, buf.at[part, pl.ds(at, span)], sems.at[c, i]))
            copies[c][-1].start(priority=1)
            at += span

    def product(low, high):
        return jnp.dot(test_buf[:, low:high], buf[low:high, :], preferred_element_type=jnp.float32)

    run_copies(copies, product, cuts, total)
    if not tables:
        outs[0][...] = total[...]
        return
    for table, out in zip(tables, outs):
        block = pick(table, me)
        place = jnp.where(block // half == me // half, half + (block - me + half) % half - 1, block % half)
        out[...] = total[:, pl.ds(pl.multiple_of(place * width, width), width)].astype(out.dtype)


def project(n, tables, out_dtype, test, inverse):
    tests, depth = test.shape[1:]
    width = inverse.shape[2] // n
    count = max(len(tables), 1)
    runs = n // 2 if tables else 1
    rows = min(depth, 2 * LANES)
    cuts = list(range(0, depth, rows)) + [depth]
    if cuts[-1] - cuts[-2] == 2 * LANES:
        cuts.insert(-1, depth - LANES)
    return pl.pallas_call(
        functools.partial(project_kernel, n, tables, cuts),
        in_specs=[ANY, ANY],
        out_specs=[VMEM] * count,
        out_shape=[jax.ShapeDtypeStruct((tests, width), out_dtype)] * count,
        scratch_shapes=[
            pltpu.VMEM((tests, depth), test.dtype),
            pltpu.VMEM((depth, width * count), inverse.dtype),
            pltpu.VMEM((tests, width * count), jnp.float32),
            pltpu.SemaphoreType.DMA((len(cuts) - 1,)),
            pltpu.SemaphoreType.DMA((len(cuts) - 1, runs)),
        ],
        compiler_params=pltpu.CompilerParams(vmem_limit_bytes=215 * MIB // 4),
        cost_estimate=pl.CostEstimate(
            flops=2 * tests * depth * width * count, bytes_accessed=2 * depth * width * count, transcendentals=0
        ),
        name="project",
    )(test, inverse)


def score_kernel(tables, parts, axes, *refs):
    count = len(tables)
    blocks, train_ref, refs = refs[:count], refs[count], refs[count + 1 :]
    me = lax.axis_index("dp")
    width = blocks[0].shape[1]
    contract = (((1,), (1,)), ((), ()))
    value = None
    for table, block in zip(tables, blocks):
        columns = pl.ds(pl.multiple_of(pick(table, me) * width, width), width)
        term = lax.dot_general(block[...], train_ref[0, :, columns], contract, preferred_element_type=jnp.float32)
        value = term if value is None else value + term
    if not parts:
        refs[-1][...] = value if len(refs) == 1 else refs[0][...] + value
        return
    so_far, weight_ref, outs, raw = refs[0], refs[1], refs[2:-1], refs[-1]
    raw[...] = (so_far[...] + value) * weight_ref[...]
    place = lax.axis_index(axes[0]) * lax.axis_size(axes[1]) + lax.axis_index(axes[1])
    rows = outs[0].shape[0]
    for step, out in enumerate(outs):
        out[...] = raw[pl.ds(pl.multiple_of(lax.bitwise_xor(place, step) * rows, rows), rows), :]


def score(tables, parts, axes, blocks, train, *more):
    tests, width = blocks[0].shape
    columns = train.shape[1]
    count = len(blocks)
    outs = max(parts, 1)
    return pl.pallas_call(
        functools.partial(score_kernel, tables, parts, axes),
        in_specs=[VMEM] * (count + 1 + len(more)),
        out_specs=[VMEM] * outs,
        out_shape=[jax.ShapeDtypeStruct((tests // outs, columns), jnp.float32)] * outs,
        scratch_shapes=[pltpu.VMEM((tests, columns), jnp.float32)] * bool(parts),
        compiler_params=pltpu.CompilerParams(vmem_limit_bytes=16 * MIB),
        cost_estimate=pl.CostEstimate(
            flops=2 * count * tests * columns * width, bytes_accessed=2 * count * columns * width, transcendentals=0
        ),
        name="score",
    )(*blocks, train, *more)


def send(x, axes, table):
    return lax.ppermute(x, axes, list(enumerate(table)))


def line_shards(n, parts, axes, test_feat, kernel_inverse, train_feat, residual_weight):
    out_tables = [folded_ring(n, step) for step in range(1, n)]
    away = project(n, out_tables, jnp.bfloat16, test_feat, kernel_inverse)
    terms = [send(block, "dp", table) for table, block in zip(out_tables, away)]
    (total,) = project(n, [], jnp.float32, test_feat, kernel_inverse)
    for term in terms:
        total = total + term
    total = total.astype(jnp.bfloat16)
    back_tables = [plain_ring(n, step) for step in range(1, n)]
    blocks = [total] + [send(total, "dp", table) for table in back_tables]
    owners = [plain_ring(n, 0)] + [sources(table) for table in back_tables]
    (raw,) = score(owners[:2], 0, axes, blocks[:2], train_feat)
    for i in range(2, n - 1):
        (raw,) = score(owners[i : i + 1], 0, axes, blocks[i : i + 1], train_feat, raw)
    rows = score(owners[n - 1 :], parts, axes, blocks[n - 1 :], train_feat, raw, residual_weight)
    result = rows[0]
    for step in (parts - 1, *range(1, parts - 1)):
        result = result + send(rows[step], axes, [z ^ step for z in range(parts)])
    return result


def general_shards(test_feat, kernel_inverse, train_feat, residual_weight):
    partial_sum = jnp.dot(test_feat[0], kernel_inverse[0], preferred_element_type=jnp.float32)
    projected = lax.psum(partial_sum, "dp").astype(jnp.bfloat16)
    raw = jnp.einsum("tf,nf->tn", projected, train_feat[0], preferred_element_type=jnp.float32)
    totals = raw * residual_weight[0][None, :]
    return lax.psum_scatter(totals, ("feat", "ens"), scatter_dimension=0, tiled=True)


def solution(mesh):
    in_specs = (
        P("ens", "groups", "dp"),
        P("ens", "dp", "feat"),
        P("ens", "dp", "feat"),
        P("ens", "dp"),
    )
    out_specs = P(("groups", "feat", "ens"), "dp")
    line, axes = mesh.shape["dp"], ("feat", "ens")
    parts = mesh.shape["feat"] * mesh.shape["ens"]
    if 2 < line <= SHORT_LINE and line % 2 == 0 and parts > 2 and parts & (parts - 1) == 0:
        body = functools.partial(line_shards, line, parts, axes)
    else:
        body = general_shards
    return jax.shard_map(body, mesh=mesh, in_specs=in_specs, out_specs=out_specs, check_vma=False)
```

```python
import functools

import jax
import jax.numpy as jnp
from jax import lax
from jax.experimental import pallas as pl
from jax.experimental.pallas import tpu as pltpu
from jax.sharding import PartitionSpec as P

VMEM = pl.BlockSpec(memory_space=pltpu.VMEM)
ANY = pl.BlockSpec(memory_space=pl.ANY)
MIB = 2**20
LANES = 128
SHORT_LINE = 4


def pick(table, z):
    value = table[0]
    for i, entry in enumerate(table[1:], 1):
        value = jnp.where(z == i, entry, value)
    return value


def sources(table):
    return tuple(table.index(i) for i in range(len(table)))


def plain_ring(n, step):
    return tuple((z + step) % n for z in range(n))


def folded_ring(n, step):
    ring = (0, *range(1, n, 2), *range(n - 2, 0, -2))
    return tuple(ring[(ring.index(z) + step) % n] for z in range(n))


def run_copies(copies, product, cuts, total):
    for c, (low, high) in enumerate(zip(cuts, cuts[1:])):
        for copy in copies[c]:
            copy.wait()
        term = product(low, high)
        total[...] = total[...] + term if c else term


def project_kernel(n, tables, cuts, test_ref, inverse_ref, *rest):
    outs, (test_buf, buf, total, test_sems, sems) = rest[:-5], rest[-5:]
    me = lax.axis_index("dp")
    width = outs[0].shape[1]
    half = n // 2
    near = me // half * half
    if tables:
        runs = [((half - near) * width, half * width)]
        runs += [((near + (me + j) % half) * width, width) for j in range(1, half)]
    else:
        runs = [(me * width, width)]
    copies = []
    for c, (low, high) in enumerate(zip(cuts, cuts[1:])):
        part = pl.ds(low, high - low)
        copies.append([pltpu.make_async_copy(test_ref.at[0, :, part], test_buf.at[:, part], test_sems.at[c])])
        copies[c][0].start()
        at = 0
        for i, (first, span) in enumerate(runs):
            source = inverse_ref.at[0, part, pl.ds(pl.multiple_of(first, span), span)]
            copies[c].append(pltpu.make_async_copy(source, buf.at[part, pl.ds(at, span)], sems.at[c, i]))
            copies[c][-1].start(priority=1)
            at += span

    def product(low, high):
        return jnp.dot(test_buf[:, low:high], buf[low:high, :], preferred_element_type=jnp.float32)

    run_copies(copies, product, cuts, total)
    if not tables:
        outs[0][...] = total[...]
        return
    for table, out in zip(tables, outs):
        block = pick(table, me)
        place = jnp.where(block // half == me // half, half + (block - me + half) % half - 1, block % half)
        out[...] = total[:, pl.ds(pl.multiple_of(place * width, width), width)].astype(out.dtype)


def project(n, tables, out_dtype, test, inverse):
    tests, depth = test.shape[1:]
    width = inverse.shape[2] // n
    count = max(len(tables), 1)
    runs = n // 2 if tables else 1
    rows = min(depth, 2 * LANES)
    cuts = list(range(0, depth, rows)) + [depth]
    if cuts[-1] - cuts[-2] == 2 * LANES:
        cuts.insert(-1, depth - LANES)
        cuts.insert(1, LANES)
    return pl.pallas_call(
        functools.partial(project_kernel, n, tables, cuts),
        in_specs=[ANY, ANY],
        out_specs=[VMEM] * count,
        out_shape=[jax.ShapeDtypeStruct((tests, width), out_dtype)] * count,
        scratch_shapes=[
            pltpu.VMEM((tests, depth), test.dtype),
            pltpu.VMEM((depth, width * count), inverse.dtype),
            pltpu.VMEM((tests, width * count), jnp.float32),
            pltpu.SemaphoreType.DMA((len(cuts) - 1,)),
            pltpu.SemaphoreType.DMA((len(cuts) - 1, runs)),
        ],
        compiler_params=pltpu.CompilerParams(vmem_limit_bytes=215 * MIB // 4),
        cost_estimate=pl.CostEstimate(
            flops=2 * tests * depth * width * count, bytes_accessed=2 * depth * width * count, transcendentals=0
        ),
        name="project",
    )(test, inverse)


def score_kernel(tables, parts, axes, *refs):
    count = len(tables)
    blocks, train_ref, refs = refs[:count], refs[count], refs[count + 1 :]
    me = lax.axis_index("dp")
    width = blocks[0].shape[1]
    contract = (((1,), (1,)), ((), ()))
    value = None
    for table, block in zip(tables, blocks):
        columns = pl.ds(pl.multiple_of(pick(table, me) * width, width), width)
        term = lax.dot_general(block[...], train_ref[0, :, columns], contract, preferred_element_type=jnp.float32)
        value = term if value is None else value + term
    if not parts:
        refs[-1][...] = value if len(refs) == 1 else refs[0][...] + value
        return
    so_far, weight_ref, outs, raw = refs[0], refs[1], refs[2:-1], refs[-1]
    raw[...] = (so_far[...] + value) * weight_ref[...]
    place = lax.axis_index(axes[0]) * lax.axis_size(axes[1]) + lax.axis_index(axes[1])
    rows = outs[0].shape[0]
    for step, out in enumerate(outs):
        out[...] = raw[pl.ds(pl.multiple_of(lax.bitwise_xor(place, step) * rows, rows), rows), :]


def score(tables, parts, axes, blocks, train, *more):
    tests, width = blocks[0].shape
    columns = train.shape[1]
    count = len(blocks)
    outs = max(parts, 1)
    return pl.pallas_call(
        functools.partial(score_kernel, tables, parts, axes),
        in_specs=[VMEM] * (count + 1 + len(more)),
        out_specs=[VMEM] * outs,
        out_shape=[jax.ShapeDtypeStruct((tests // outs, columns), jnp.float32)] * outs,
        scratch_shapes=[pltpu.VMEM((tests, columns), jnp.float32)] * bool(parts),
        compiler_params=pltpu.CompilerParams(vmem_limit_bytes=16 * MIB),
        cost_estimate=pl.CostEstimate(
            flops=2 * count * tests * columns * width, bytes_accessed=2 * count * columns * width, transcendentals=0
        ),
        name="score",
    )(*blocks, train, *more)


def send(x, axes, table):
    return lax.ppermute(x, axes, list(enumerate(table)))


def line_shards(n, parts, axes, test_feat, kernel_inverse, train_feat, residual_weight):
    out_tables = [folded_ring(n, step) for step in range(1, n)]
    away = project(n, out_tables, jnp.bfloat16, test_feat, kernel_inverse)
    terms = [send(block, "dp", table) for table, block in zip(out_tables, away)]
    (total,) = project(n, [], jnp.float32, test_feat, kernel_inverse)
    for term in terms:
        total = total + term
    total = total.astype(jnp.bfloat16)
    back_tables = [plain_ring(n, step) for step in range(1, n)]
    blocks = [total] + [send(total, "dp", table) for table in back_tables]
    owners = [plain_ring(n, 0)] + [sources(table) for table in back_tables]
    (raw,) = score(owners[:2], 0, axes, blocks[:2], train_feat)
    for i in range(2, n - 1):
        (raw,) = score(owners[i : i + 1], 0, axes, blocks[i : i + 1], train_feat, raw)
    rows = score(owners[n - 1 :], parts, axes, blocks[n - 1 :], train_feat, raw, residual_weight)
    result = rows[0]
    for step in (parts - 1, *range(1, parts - 1)):
        result = result + send(rows[step], axes, [z ^ step for z in range(parts)])
    return result


def general_shards(test_feat, kernel_inverse, train_feat, residual_weight):
    partial_sum = jnp.dot(test_feat[0], kernel_inverse[0], preferred_element_type=jnp.float32)
    projected = lax.psum(partial_sum, "dp").astype(jnp.bfloat16)
    raw = jnp.einsum("tf,nf->tn", projected, train_feat[0], preferred_element_type=jnp.float32)
    totals = raw * residual_weight[0][None, :]
    return lax.psum_scatter(totals, ("feat", "ens"), scatter_dimension=0, tiled=True)


def solution(mesh):
    in_specs = (
        P("ens", "groups", "dp"),
        P("ens", "dp", "feat"),
        P("ens", "dp", "feat"),
        P("ens", "dp"),
    )
    out_specs = P(("groups", "feat", "ens"), "dp")
    line, axes = mesh.shape["dp"], ("feat", "ens")
    parts = mesh.shape["feat"] * mesh.shape["ens"]
    if 2 < line <= SHORT_LINE and line % 2 == 0 and parts > 2 and parts & (parts - 1) == 0:
        body = functools.partial(line_shards, line, parts, axes)
    else:
        body = general_shards
    return jax.shard_map(body, mesh=mesh, in_specs=in_specs, out_specs=out_specs, check_vma=False)
```

```python
import functools

import jax
import jax.numpy as jnp
from jax import lax
from jax.experimental import pallas as pl
from jax.experimental.pallas import tpu as pltpu
from jax.sharding import PartitionSpec as P

VMEM = pl.BlockSpec(memory_space=pltpu.VMEM)
ANY = pl.BlockSpec(memory_space=pl.ANY)
MIB = 2**20
LANES = 128
SHORT_LINE = 4


def pick(table, z):
    value = table[0]
    for i, entry in enumerate(table[1:], 1):
        value = jnp.where(z == i, entry, value)
    return value


def sources(table):
    return tuple(table.index(i) for i in range(len(table)))


def plain_ring(n, step):
    return tuple((z + step) % n for z in range(n))


def folded_ring(n, step):
    ring = (0, *range(1, n, 2), *range(n - 2, 0, -2))
    return tuple(ring[(ring.index(z) + step) % n] for z in range(n))


def run_copies(copies, product, cuts, total):
    for c, (low, high) in enumerate(zip(cuts, cuts[1:])):
        for copy in copies[c]:
            copy.wait()
        term = product(low, high)
        total[...] = total[...] + term if c else term


def project_kernel(n, tables, cuts, test_ref, inverse_ref, *rest):
    outs, (test_buf, buf, total, test_sems, sems) = rest[:-5], rest[-5:]
    me = lax.axis_index("dp")
    width = outs[0].shape[1]
    half = n // 2
    near = me // half * half
    if tables:
        runs = [((half - near) * width, half * width)]
        runs += [((near + (me + j) % half) * width, width) for j in range(1, half)]
    else:
        runs = [(me * width, width)]
    copies = []
    for c, (low, high) in enumerate(zip(cuts, cuts[1:])):
        part = pl.ds(low, high - low)
        copies.append([pltpu.make_async_copy(test_ref.at[0, :, part], test_buf.at[:, part], test_sems.at[c])])
        copies[c][0].start()
        at = 0
        for i, (first, span) in enumerate(runs):
            source = inverse_ref.at[0, part, pl.ds(pl.multiple_of(first, span), span)]
            copies[c].append(pltpu.make_async_copy(source, buf.at[part, pl.ds(at, span)], sems.at[c, i]))
            copies[c][-1].start(priority=1)
            at += span

    def product(low, high):
        return jnp.dot(test_buf[:, low:high], buf[low:high, :], preferred_element_type=jnp.float32)

    run_copies(copies, product, cuts, total)
    if not tables:
        outs[0][...] = total[...]
        return
    for table, out in zip(tables, outs):
        block = pick(table, me)
        place = jnp.where(block // half == me // half, half + (block - me + half) % half - 1, block % half)
        out[...] = total[:, pl.ds(pl.multiple_of(place * width, width), width)].astype(out.dtype)


def project(n, tables, out_dtype, test, inverse):
    tests, depth = test.shape[1:]
    width = inverse.shape[2] // n
    count = max(len(tables), 1)
    runs = n // 2 if tables else 1
    rows = min(depth, 2 * LANES)
    cuts = list(range(0, depth, rows)) + [depth]
    if cuts[-1] - cuts[-2] == 2 * LANES:
        cuts.insert(-1, depth - LANES)
        cuts.insert(1, LANES)
    return pl.pallas_call(
        functools.partial(project_kernel, n, tables, cuts),
        in_specs=[ANY, ANY],
        out_specs=[VMEM] * count,
        out_shape=[jax.ShapeDtypeStruct((tests, width), out_dtype)] * count,
        scratch_shapes=[
            pltpu.VMEM((tests, depth), test.dtype),
            pltpu.VMEM((depth, width * count), inverse.dtype),
            pltpu.VMEM((tests, width * count), jnp.float32),
            pltpu.SemaphoreType.DMA((len(cuts) - 1,)),
            pltpu.SemaphoreType.DMA((len(cuts) - 1, runs)),
        ],
        compiler_params=pltpu.CompilerParams(vmem_limit_bytes=215 * MIB // 4),
        cost_estimate=pl.CostEstimate(
            flops=2 * tests * depth * width * count, bytes_accessed=2 * depth * width * count, transcendentals=0
        ),
        name="project",
    )(test, inverse)


def score_kernel(tables, parts, axes, *refs):
    count = len(tables)
    blocks, train_ref, refs = refs[:count], refs[count], refs[count + 1 :]
    me = lax.axis_index("dp")
    width = blocks[0].shape[1]
    contract = (((1,), (1,)), ((), ()))
    value = None
    for table, block in zip(tables, blocks):
        columns = pl.ds(pl.multiple_of(pick(table, me) * width, width), width)
        term = lax.dot_general(block[...], train_ref[0, :, columns], contract, preferred_element_type=jnp.float32)
        value = term if value is None else value + term
    if not parts:
        refs[-1][...] = value if len(refs) == 1 else refs[0][...] + value
        return
    so_far, weight_ref, outs, raw = refs[0], refs[1], refs[2:-1], refs[-1]
    raw[...] = (so_far[...] + value) * weight_ref[...]
    place = lax.axis_index(axes[0]) * lax.axis_size(axes[1]) + lax.axis_index(axes[1])
    rows = outs[0].shape[0]
    for step, out in enumerate(outs):
        out[...] = raw[pl.ds(pl.multiple_of(lax.bitwise_xor(place, step) * rows, rows), rows), :]


def score(tables, parts, axes, blocks, train, *more):
    tests, width = blocks[0].shape
    columns = train.shape[1]
    count = len(blocks)
    outs = max(parts, 1)
    return pl.pallas_call(
        functools.partial(score_kernel, tables, parts, axes),
        in_specs=[VMEM] * (count + 1 + len(more)),
        out_specs=[VMEM] * outs,
        out_shape=[jax.ShapeDtypeStruct((tests // outs, columns), jnp.float32)] * outs,
        scratch_shapes=[pltpu.VMEM((tests, columns), jnp.float32)] * bool(parts),
        compiler_params=pltpu.CompilerParams(vmem_limit_bytes=16 * MIB),
        cost_estimate=pl.CostEstimate(
            flops=2 * count * tests * columns * width, bytes_accessed=2 * count * columns * width, transcendentals=0
        ),
        name="score",
    )(*blocks, train, *more)


def send(x, axes, table):
    return lax.ppermute(x, axes, list(enumerate(table)))


def line_shards(n, parts, axes, test_feat, kernel_inverse, train_feat, residual_weight):
    out_tables = [folded_ring(n, step) for step in range(1, n)]
    away = project(n, out_tables, jnp.bfloat16, test_feat, kernel_inverse)
    terms = [send(block, "dp", table) for table, block in zip(out_tables, away)]
    (total,) = project(n, [], jnp.float32, test_feat, kernel_inverse)
    total = sum(terms[1:], terms[0].astype(jnp.float32)) + total
    total = total.astype(jnp.bfloat16)
    back_tables = [plain_ring(n, step) for step in range(1, n)]
    blocks = [total] + [send(total, "dp", table) for table in back_tables]
    owners = [plain_ring(n, 0)] + [sources(table) for table in back_tables]
    (raw,) = score(owners[:2], 0, axes, blocks[:2], train_feat)
    for i in range(2, n - 1):
        (raw,) = score(owners[i : i + 1], 0, axes, blocks[i : i + 1], train_feat, raw)
    rows = score(owners[n - 1 :], parts, axes, blocks[n - 1 :], train_feat, raw, residual_weight)
    result = rows[0]
    for step in (parts - 1, *range(1, parts - 1)):
        result = result + send(rows[step], axes, [z ^ step for z in range(parts)])
    return result


def general_shards(test_feat, kernel_inverse, train_feat, residual_weight):
    partial_sum = jnp.dot(test_feat[0], kernel_inverse[0], preferred_element_type=jnp.float32)
    projected = lax.psum(partial_sum, "dp").astype(jnp.bfloat16)
    raw = jnp.einsum("tf,nf->tn", projected, train_feat[0], preferred_element_type=jnp.float32)
    totals = raw * residual_weight[0][None, :]
    return lax.psum_scatter(totals, ("feat", "ens"), scatter_dimension=0, tiled=True)


def solution(mesh):
    in_specs = (
        P("ens", "groups", "dp"),
        P("ens", "dp", "feat"),
        P("ens", "dp", "feat"),
        P("ens", "dp"),
    )
    out_specs = P(("groups", "feat", "ens"), "dp")
    line, axes = mesh.shape["dp"], ("feat", "ens")
    parts = mesh.shape["feat"] * mesh.shape["ens"]
    if 2 < line <= SHORT_LINE and line % 2 == 0 and parts > 2 and parts & (parts - 1) == 0:
        body = functools.partial(line_shards, line, parts, axes)
    else:
        body = general_shards
    return jax.shard_map(body, mesh=mesh, in_specs=in_specs, out_specs=out_specs, check_vma=False)
```

```python
import functools

import jax
import jax.numpy as jnp
from jax import lax
from jax.experimental import pallas as pl
from jax.experimental.pallas import tpu as pltpu
from jax.sharding import PartitionSpec as P

VMEM = pl.BlockSpec(memory_space=pltpu.VMEM)
ANY = pl.BlockSpec(memory_space=pl.ANY)
MIB = 2**20
LANES = 128
SHORT_LINE = 4


def pick(table, z):
    value = table[0]
    for i, entry in enumerate(table[1:], 1):
        value = jnp.where(z == i, entry, value)
    return value


def sources(table):
    return tuple(table.index(i) for i in range(len(table)))


def plain_ring(n, step):
    return tuple((z + step) % n for z in range(n))


def folded_ring(n, step):
    ring = (0, *range(1, n, 2), *range(n - 2, 0, -2))
    return tuple(ring[(ring.index(z) + step) % n] for z in range(n))


def run_copies(copies, product, cuts, total):
    for c, (low, high) in enumerate(zip(cuts, cuts[1:])):
        for copy in copies[c]:
            copy.wait()
        term = product(low, high)
        total[...] = total[...] + term if c else term


def project_kernel(n, tables, cuts, test_ref, inverse_ref, *rest):
    outs, (test_buf, buf, total, test_sems, sems) = rest[:-5], rest[-5:]
    me = lax.axis_index("dp")
    width = outs[0].shape[1]
    half = n // 2
    near = me // half * half
    if tables:
        runs = [((half - near) * width, half * width)]
        runs += [((near + (me + j) % half) * width, width) for j in range(1, half)]
    else:
        runs = [(me * width, width)]
    copies = []
    for c, (low, high) in enumerate(zip(cuts, cuts[1:])):
        part = pl.ds(low, high - low)
        copies.append([pltpu.make_async_copy(test_ref.at[0, :, part], test_buf.at[:, part], test_sems.at[c])])
        copies[c][0].start()
        at = 0
        for i, (first, span) in enumerate(runs):
            source = inverse_ref.at[0, part, pl.ds(pl.multiple_of(first, span), span)]
            copies[c].append(pltpu.make_async_copy(source, buf.at[part, pl.ds(at, span)], sems.at[c, i]))
            copies[c][-1].start(priority=1)
            at += span

    def product(low, high):
        return jnp.dot(test_buf[:, low:high], buf[low:high, :], preferred_element_type=jnp.float32)

    run_copies(copies, product, cuts, total)
    if not tables:
        outs[0][...] = total[...]
        return
    for table, out in zip(tables, outs):
        block = pick(table, me)
        place = jnp.where(block // half == me // half, half + (block - me + half) % half - 1, block % half)
        out[...] = total[:, pl.ds(pl.multiple_of(place * width, width), width)].astype(out.dtype)


def project(n, tables, out_dtype, test, inverse):
    tests, depth = test.shape[1:]
    width = inverse.shape[2] // n
    count = max(len(tables), 1)
    runs = n // 2 if tables else 1
    rows = min(depth, 2 * LANES)
    cuts = list(range(0, depth, rows)) + [depth]
    if cuts[-1] - cuts[-2] == 2 * LANES:
        cuts.insert(-1, depth - LANES)
        cuts.insert(1, LANES)
    return pl.pallas_call(
        functools.partial(project_kernel, n, tables, cuts),
        in_specs=[ANY, ANY],
        out_specs=[VMEM] * count,
        out_shape=[jax.ShapeDtypeStruct((tests, width), out_dtype)] * count,
        scratch_shapes=[
            pltpu.VMEM((tests, depth), test.dtype),
            pltpu.VMEM((depth, width * count), inverse.dtype),
            pltpu.VMEM((tests, width * count), jnp.float32),
            pltpu.SemaphoreType.DMA((len(cuts) - 1,)),
            pltpu.SemaphoreType.DMA((len(cuts) - 1, runs)),
        ],
        compiler_params=pltpu.CompilerParams(vmem_limit_bytes=215 * MIB // 4),
        cost_estimate=pl.CostEstimate(
            flops=2 * tests * depth * width * count, bytes_accessed=2 * depth * width * count, transcendentals=0
        ),
        name="project",
    )(test, inverse)


def score_kernel(tables, parts, axes, *refs):
    count = len(tables)
    blocks, train_ref, refs = refs[:count], refs[count], refs[count + 1 :]
    me = lax.axis_index("dp")
    width = blocks[0].shape[1]
    contract = (((1,), (1,)), ((), ()))
    value = None
    for table, block in zip(tables, blocks):
        columns = pl.ds(pl.multiple_of(pick(table, me) * width, width), width)
        term = lax.dot_general(block[...], train_ref[0, :, columns], contract, preferred_element_type=jnp.float32)
        value = term if value is None else value + term
    if not parts:
        refs[-1][...] = value if len(refs) == 1 else refs[0][...] + value
        return
    so_far, weight_ref, outs, raw = refs[0], refs[1], refs[2:-1], refs[-1]
    raw[...] = (so_far[...] + value) * weight_ref[...]
    place = lax.axis_index(axes[0]) * lax.axis_size(axes[1]) + lax.axis_index(axes[1])
    rows = outs[0].shape[0]
    for step, out in enumerate(outs):
        out[...] = raw[pl.ds(pl.multiple_of(lax.bitwise_xor(place, step) * rows, rows), rows), :]


def score(tables, parts, axes, blocks, train, *more):
    tests, width = blocks[0].shape
    columns = train.shape[1]
    count = len(blocks)
    outs = max(parts, 1)
    return pl.pallas_call(
        functools.partial(score_kernel, tables, parts, axes),
        in_specs=[VMEM] * (count + 1 + len(more)),
        out_specs=[VMEM] * outs,
        out_shape=[jax.ShapeDtypeStruct((tests // outs, columns), jnp.float32)] * outs,
        scratch_shapes=[pltpu.VMEM((tests, columns), jnp.float32)] * bool(parts),
        compiler_params=pltpu.CompilerParams(vmem_limit_bytes=16 * MIB),
        cost_estimate=pl.CostEstimate(
            flops=2 * count * tests * columns * width, bytes_accessed=2 * count * columns * width, transcendentals=0
        ),
        name="score",
    )(*blocks, train, *more)


def send(x, axes, table):
    return lax.ppermute(x, axes, list(enumerate(table)))


def line_shards(n, parts, axes, test_feat, kernel_inverse, train_feat, residual_weight):
    out_tables = [folded_ring(n, step) for step in range(1, n)]
    away = project(n, out_tables, jnp.bfloat16, test_feat, kernel_inverse)
    terms = [send(block, "dp", table) for table, block in zip(out_tables, away)]
    (total,) = project(n, [], jnp.float32, test_feat, kernel_inverse)
    for term in terms:
        total = total + term
    total = total.astype(jnp.bfloat16)
    back_tables = [plain_ring(n, step) for step in range(1, n)]
    blocks = [total] + [send(total, "dp", table) for table in back_tables]
    owners = [plain_ring(n, 0)] + [sources(table) for table in back_tables]
    (raw,) = score(owners[:1], 0, axes, blocks[:1], train_feat)
    for i in range(1, n - 1):
        (raw,) = score(owners[i : i + 1], 0, axes, blocks[i : i + 1], train_feat, raw)
    rows = score(owners[n - 1 :], parts, axes, blocks[n - 1 :], train_feat, raw, residual_weight)
    result = rows[0]
    for step in (parts - 1, *range(1, parts - 1)):
        result = result + send(rows[step], axes, [z ^ step for z in range(parts)])
    return result


def general_shards(test_feat, kernel_inverse, train_feat, residual_weight):
    partial_sum = jnp.dot(test_feat[0], kernel_inverse[0], preferred_element_type=jnp.float32)
    projected = lax.psum(partial_sum, "dp").astype(jnp.bfloat16)
    raw = jnp.einsum("tf,nf->tn", projected, train_feat[0], preferred_element_type=jnp.float32)
    totals = raw * residual_weight[0][None, :]
    return lax.psum_scatter(totals, ("feat", "ens"), scatter_dimension=0, tiled=True)


def solution(mesh):
    in_specs = (
        P("ens", "groups", "dp"),
        P("ens", "dp", "feat"),
        P("ens", "dp", "feat"),
        P("ens", "dp"),
    )
    out_specs = P(("groups", "feat", "ens"), "dp")
    line, axes = mesh.shape["dp"], ("feat", "ens")
    parts = mesh.shape["feat"] * mesh.shape["ens"]
    if 2 < line <= SHORT_LINE and line % 2 == 0 and parts > 2 and parts & (parts - 1) == 0:
        body = functools.partial(line_shards, line, parts, axes)
    else:
        body = general_shards
    return jax.shard_map(body, mesh=mesh, in_specs=in_specs, out_specs=out_specs, check_vma=False)
```
